512 devices in a mesh: ep: 64 (over y, z), dp: 8 (over x, core).
Axes of the slice: x: 4, y: 8, z: 8, core: 2. Of those that a mesh axis runs over, the one named last changes fastest.
Arguments:
- tokens: bfloat16 [8192, 4096], P('ep', 'dp'), may hold values from -6 to 6
- routing: int32 [8192, 8], P('ep'), may hold values from 0 to 255, all different within a row; in each aligned block of 128 rows (0 to 127, 128 to 255, ...) at most 8 rows name the same one
- w_gate: bfloat16 [64, 4096, 1024], P('ep', 'dp'), may hold values from -0.09375 to 0.09375
- w_up: bfloat16 [64, 4096, 1024], P('ep', 'dp'), may hold values from -0.09375 to 0.09375
- cotangent: bfloat16 [8192, 8, 1024], P('ep', None, 'dp'), may hold values from -6 to 6
Outputs:
- hidden: bfloat16 [8192, 8, 1024], P('ep', None, 'dp')
- input_grad: bfloat16 [8192, 4096], P('ep', 'dp')
- grad_gate: bfloat16 [64, 4096, 1024], P('ep', 'dp')
- grad_up: bfloat16 [64, 4096, 1024], P('ep', 'dp')
The draws below stay inside these ranges and needn't reach their ends.
Inputs may be any that keep to these rules, and one draw needn't show every extreme that they name: `routing`: the 8 experts of a token are different. In each aligned block of 128 rows (the rows of one index of ep) no expert is named by more than 8 rows, a bound that some block reaches.
All inputs are finite; a program needn't handle non-finite values.
Results may differ from the reference program's by a relative error of at most 0.025.
Values may be sent and summed in bfloat16 or wider, within the bound.
A program may use at most 64 MiB of HBM per device.

```python
import math
import jax
import jax.numpy as jnp
import numpy as np
from jax import lax

D = 4096
H = 1024
TOPK = 8
TOK_DEV = 128
EXPERTS = 64
ALL_EXPERTS = 256
CAP = 8
TOKENS = 8192
N_DP = 8


def steps_of(own_key, extent, shards, least, high):
    def one(axis_at, parts):
        steps = jax.random.uniform(jax.random.fold_in(jax.random.fold_in(own_key, 6), axis_at), (parts,), jnp.float32, least / len(shards), high / len(shards))
        return jnp.repeat(jnp.exp(steps), extent[axis_at] // parts).reshape((-1,) + (1,) * (len(extent) - axis_at - 1))

    factor_of = one(*shards[0])
    for cut in shards[1:]:
        factor_of = factor_of * one(*cut)
    return factor_of


def assign_block(rng, own, number, rows, count, top, limit, skew):
    order = jax.random.permutation(rng, count)
    packed, ordinary = load_shares(count, rows * top, limit, skew, True), load_shares(count, rows * top, limit, skew, False)
    places = jnp.arange(count)

    def named(sizes, offset_by):
        used = int((sizes > 0).sum())
        fixed = max(1, used // 4)
        moved = fixed + (places - fixed + offset_by * (used - fixed)) % max(1, count - fixed)
        return jnp.zeros((count,), jnp.int32).at[order[jnp.where(places < fixed, places, moved)]].set(jnp.asarray(sizes, jnp.int32))

    sizes = jnp.where(number % 4 == 0, named(packed, number // 4), named(ordinary, number - number // 4 - 1))
    mixed = jax.random.permutation(jax.random.fold_in(own, 3), count)
    source_of, receiver = mixed[0:count // 2 * 2:2], mixed[1:count // 2 * 2:2]
    room = jnp.minimum(sizes[source_of] - 1, limit - sizes[receiver]) // 2
    room = jnp.where((source_of == order[0]) | (receiver == order[0]) | (sizes[receiver] == 0), 0, jnp.maximum(room, 0))
    moved = jax.random.randint(jax.random.fold_in(own, 4), (count // 2,), 0, 1 << 20) % (room + 1)
    sizes = sizes.at[source_of].add(-moved).at[receiver].add(moved)
    items = jnp.searchsorted(jnp.cumsum(sizes), jnp.arange(rows * top), side="right").astype(jnp.int32)
    table = items.reshape(top, rows).T
    table = table[jax.random.permutation(jax.random.fold_in(own, 1), rows)]
    offset_by = jax.random.randint(jax.random.fold_in(own, 2), (rows, 1), 0, top)
    return jnp.take_along_axis(table, (jnp.arange(top)[None, :] + offset_by) % top, axis=1)


def load_shares(number_of, total, limit, skew, full):
    portions = [(1 << 20) // math.isqrt(rank ** skew) + 1 for rank in range(1, number_of + 1)]
    largest = limit if full else min(limit, max(-(-total // number_of), total * portions[0] // sum(portions)))
    least = 1 if total - largest >= number_of - 1 else 0
    given, spare = [largest] + [least] * (number_of - 1), total - largest - least * (number_of - 1)
    while spare > 0:
        movable = [i for i in range(1, number_of) if given[i] < largest] or [i for i in range(1, number_of) if given[i] < limit]
        pool, left = sum([portions[i] for i in movable]), spare
        for i in movable:
            addition = min(limit - given[i], max(1, left * portions[i] // pool), spare)
            given[i] = given[i] + addition
            spare = spare - addition
    return np.array(given)


def normal_values(key, shape, spread, bound, pieces=(), held_as=jnp.bfloat16):
    drawn = spread * jax.random.normal(key, shape, jnp.float32)
    if pieces:
        drawn = drawn * steps_of(key, shape, pieces, -0.22, 0.18)
    return jnp.clip(drawn, -bound, bound).astype(held_as)


def setup_inputs(seed: int = 0) -> dict:
    key_list = jax.random.split(jax.random.key(seed), 6)
    tokens = normal_values(key_list[0], (TOKENS, D), 1.0, 6.0, ((0, 64), (1, 8)))
    routing_keys = jax.random.split(jax.random.fold_in(key_list[1], 1), TOKENS // TOK_DEV)
    routing_turns = jax.random.permutation(jax.random.fold_in(key_list[1], 3), TOKENS // TOK_DEV)
    routing = jax.vmap(lambda own, number: assign_block(jax.random.fold_in(key_list[1], 2), own, number, TOK_DEV, ALL_EXPERTS, TOPK, CAP, 2))(routing_keys, routing_turns).reshape((TOKENS, TOPK))
    w_gate = normal_values(key_list[2], (EXPERTS, D, H), D ** -0.5, 0.09375, ((0, 64), (1, 8)))
    w_up = normal_values(key_list[3], (EXPERTS, D, H), D ** -0.5, 0.09375, ((0, 64), (1, 8)))
    cotangent = normal_values(key_list[4], (TOKENS, TOPK, H), 1.0, 6.0, ((0, 64), (2, 8)))
    return dict(tokens=tokens, routing=routing, w_gate=w_gate, w_up=w_up, cotangent=cotangent)


def swiglu_forward(preact, hidden_width):
    gate_pre = preact[:, :hidden_width]
    up_pre = preact[:, hidden_width:]
    return (gate_pre * jax.nn.sigmoid(gate_pre) * up_pre).astype(jnp.bfloat16)


def swiglu_grads(preact, upstream):
    hidden_width = upstream.shape[1]
    gate_pre = preact[:, :hidden_width]
    up_pre = preact[:, hidden_width:]
    sigmoid_gate = jax.nn.sigmoid(gate_pre)
    upstream_f = upstream.astype(jnp.float32)
    d_gate = (upstream_f * up_pre * sigmoid_gate * (1.0 + gate_pre * (1.0 - sigmoid_gate))).astype(jnp.bfloat16)
    d_up = (upstream_f * gate_pre * sigmoid_gate).astype(jnp.bfloat16)
    return jnp.concatenate([d_gate, d_up], axis=1)


def reference(tokens, routing, w_gate, w_up, cotangent):
    blocks = TOKENS // TOK_DEV
    per_block = TOK_DEV * TOPK
    feature_share = D // N_DP
    chosen = routing.reshape(blocks, per_block).astype(jnp.int32)
    onehot = (chosen[:, :, None] == jnp.arange(EXPERTS, dtype=jnp.int32)[None, None, :]).astype(jnp.int32)
    slot_index = jnp.sum((jnp.cumsum(onehot, axis=1) - onehot) * onehot, axis=2).astype(jnp.int32)
    block_ids = jnp.broadcast_to(jnp.arange(blocks, dtype=jnp.int32)[:, None], (blocks, per_block))
    pair_ids = jnp.arange(blocks * per_block, dtype=jnp.int32).reshape(blocks, per_block)
    slot_table = jnp.full((EXPERTS, blocks, CAP), -1, jnp.int32).at[chosen, block_ids, slot_index].set(
        pair_ids, mode="drop")
    flat_cot = cotangent.reshape(TOKENS * TOPK, H)
    contract_rows = (((0,), (0,)), ((), ()))
    contract_cols = (((1,), (1,)), ((), ()))

    def per_expert(totals, inputs):
        hidden_acc, grad_acc = totals
        pair_list, gate_weight, up_weight = inputs
        pair_list = pair_list.reshape(-1)
        live_rows = pair_list >= 0
        safe_ids = jnp.where(live_rows, pair_list, 0)
        routed_rows = jnp.where(live_rows[:, None], tokens[safe_ids // TOPK], jnp.zeros((), jnp.bfloat16))
        weights = jnp.concatenate([gate_weight, up_weight], axis=1)
        preact = jnp.zeros((routed_rows.shape[0], 2 * H), jnp.float32)
        for shard_index in range(N_DP):
            low = shard_index * feature_share
            block_term = jnp.dot(routed_rows[:, low:low + feature_share], weights[low:low + feature_share],
                                 preferred_element_type=jnp.float32).astype(jnp.bfloat16)
            preact = preact + lax.optimization_barrier(block_term).astype(jnp.float32)
        hidden_rows = swiglu_forward(preact, H)
        upstream = jnp.where(live_rows[:, None], flat_cot[safe_ids], jnp.zeros((), jnp.bfloat16))
        d_pair = swiglu_grads(preact, upstream)
        grad_weight = lax.dot_general(routed_rows, d_pair, contract_rows,
                                      preferred_element_type=jnp.float32).astype(jnp.bfloat16)
        pair_grad = lax.dot_general(d_pair, weights, contract_cols,
                                    preferred_element_type=jnp.float32).astype(jnp.bfloat16)
        target = jnp.where(live_rows, pair_list, TOKENS * TOPK)
        hidden_acc = hidden_acc.at[target].set(hidden_rows, mode="drop")
        token_target = jnp.where(live_rows, pair_list // TOPK, TOKENS)
        grad_acc = grad_acc.at[token_target].add(pair_grad.astype(jnp.float32), mode="drop")
        return (hidden_acc, grad_acc), (grad_weight[:, :H], grad_weight[:, H:])

    start_carry = (jnp.zeros((TOKENS * TOPK, H), jnp.bfloat16), jnp.zeros((TOKENS, D), jnp.float32))
    (hidden_all, grad_all), (grad_gate, grad_up) = lax.scan(per_expert, start_carry, (slot_table, w_gate, w_up))
    return hidden_all.reshape(TOKENS, TOPK, H), grad_all.astype(jnp.bfloat16), grad_gate, grad_up
```

```python
import functools
import math

import jax
import jax.numpy as jnp
from jax import lax
from jax.experimental import pallas as pl
from jax.experimental.pallas import tpu as pltpu
from jax.sharding import PartitionSpec as P

MESH = pl.DeviceIdType.MESH
BF16 = jnp.bfloat16
F32 = jnp.float32
CAP = 8
CHUNKS = 4


def dot(a, b, dims=(((1,), (0,)), ((), ()))):
    return lax.dot_general(a, b, dims, preferred_element_type=F32)


def fold(i, n):
    c, p = i // 2, i % 2
    moved = (c + n - 1) // n
    return (1 - p) * c + p * (n - c) - p * (n // 2) * (1 - moved)


def fold_vector(i, n):
    c, p = i >> 1, i & 1
    return jnp.where(p == 0, c, jnp.where(c == 0, n // 2, n - c))


def kernel(
    ny, nz, nx,
    tok_hbm, rout_hbm, wg_hbm, wu_hbm, cot_hbm,
    hid_out, dx_out, gg_out, gu_out,
    tok, rout, cot, w, send_d, recv_d, sel_t, sel_p, sel_pt,
    own_a, send_a, recv_a, own_b, send_b, recv_b, d_pair, send_r, recv_r, hid, grad, hid_v, dx_v,
    in_sem, w_sem, sd_sem, rd_sem, sa_sem, ra_sem, sb_sem, rb_sem, sg_sem, rg_sem, sh_sem, rh_sem,
    sr_sem, rr_sem, out_sem,
):
    experts = ny * nz
    tokens, features = tok.shape
    top = rout.shape[0]
    pairs = cot.shape[0]
    part = cot.shape[1]
    group = experts // CHUNKS
    rows = group * CAP
    me, mine = lax.axis_index("ep"), lax.axis_index("dp")
    y, z = me // nz, me % nz
    x, core = mine // 2, mine % 2
    partner = x * 2 + 1 - core

    def along_x(step):
        return (x + step) % nx * 2 + core

    def block_of(k):
        return along_x(k) if k < nx else (x + k - nx) % nx * 2 + 1 - core

    def to_expert(o):
        dy, dz = fold(o // nz, ny), fold(o % nz, nz)
        return (y + dy) % ny * nz + (z + dz) % nz

    def to_source(o):
        dy, dz = fold(o // nz, ny), fold(o % nz, nz)
        return (y + ny - dy) % ny * nz + (z + nz - dz) % nz

    small = [
        pltpu.make_async_copy(rout_hbm, rout, in_sem.at[0]),
        pltpu.make_async_copy(tok_hbm, tok, in_sem.at[1]),
        pltpu.make_async_copy(cot_hbm, cot, in_sem.at[2]),
    ]
    for copy in small:
        copy.start()
    w_copies = []
    for k in range(2 * nx):
        at = pl.ds(pl.multiple_of(block_of(k) * part, part), part)
        for n, source in enumerate((wg_hbm, wu_hbm)):
            copy = pltpu.make_async_copy(source.at[0, :, at], w.at[k, :, pl.ds(n * part, part)], w_sem.at[k, n])
            copy.start()
            w_copies.append(copy)

    barrier = pltpu.get_barrier_semaphore()

    @pl.loop(1, experts)
    def _(o):
        pl.semaphore_signal(barrier, inc=1, device_id=(to_expert(o), mine), device_id_type=MESH)

    for step in range(1, nx):
        pl.semaphore_signal(barrier, inc=1, device_id=(me, along_x(step)), device_id_type=MESH)
    pl.semaphore_signal(barrier, inc=1, device_id=(me, partner), device_id_type=MESH)

    small[0].wait()
    routes = rout[...]
    before = (
        lax.broadcasted_iota(jnp.int32, (tokens, tokens), 0) < lax.broadcasted_iota(jnp.int32, (tokens, tokens), 1)
    ).astype(F32).astype(BF16)
    spread = (
        lax.broadcasted_iota(jnp.int32, (tokens, pairs), 1) // top == lax.broadcasted_iota(jnp.int32, (tokens, pairs), 0)
    ).astype(F32).astype(BF16)
    named = dot(routes.astype(F32).astype(BF16), spread)
    place = lax.broadcasted_iota(jnp.int32, (top, pairs), 1) % top == lax.broadcasted_iota(jnp.int32, (top, pairs), 0)
    chosen = jnp.sum(jnp.where(place, named, 0.0), axis=0, keepdims=True)
    small[1].wait()
    small[2].wait()
    for c in range(CHUNKS):
        row = lax.broadcasted_iota(jnp.int32, (rows, tokens), 0)
        o = row // CAP + c * group
        dy, dz = fold_vector(o // nz, ny), fold_vector(o % nz, nz)
        expert = ((y + dy) & (ny - 1)) * nz + ((z + dz) & (nz - 1))
        slot = (row % CAP).astype(F32)
        hit = routes[0:1, :] == expert
        for k in range(1, top):
            hit = hit | (routes[k : k + 1, :] == expert)
        hit = hit.astype(F32)
        earlier = dot(hit.astype(BF16), before)
        sel = jnp.where(earlier == slot, hit, 0.0)
        picked = sel.astype(BF16)
        out_tok = dot(picked, tok[...]).astype(BF16)
        expanded = dot(picked, spread)
        expert_p = expert.astype(F32)[:, 0:1]
        sel_pair = jnp.where((chosen == expert_p), expanded, 0.0).astype(BF16)
        out_cot = dot(sel_pair, cot[...]).astype(BF16)
        outgoing = jnp.concatenate([out_tok, out_cot], axis=1).reshape(group, CAP, features + part)
        send_d[c * group : (c + 1) * group] = outgoing
        if c == 0:
            recv_d[0:1] = outgoing[0:1]
            pl.semaphore_wait(barrier, experts + nx - 1)

        @pl.loop(max(1, c * group), (c + 1) * group)
        def _(o):
            pltpu.make_async_remote_copy(
                src_ref=send_d.at[o],
                dst_ref=recv_d.at[o],
                send_sem=sd_sem.at[c],
                recv_sem=rd_sem.at[c],
                device_id=(to_expert(o), mine),
                device_id_type=MESH,
            ).start()

        sel_t[c] = sel.T.astype(BF16)
        sel_p[c] = sel_pair

    for c in range(CHUNKS):
        sel_pt[c] = sel_p[c].astype(F32).T.astype(BF16)
    for copy in w_copies:
        copy.wait()

    def wait_for(ref, sem):
        pltpu.make_async_copy(ref, ref, sem).wait()

    def remote(source, target, send_sem, recv_sem, device):
        pltpu.make_async_remote_copy(
            src_ref=source,
            dst_ref=target,
            send_sem=send_sem,
            recv_sem=recv_sem,
            device_id=(me, device),
            device_id_type=MESH,
        ).start()

    def span(c):
        first = max(1, c * group)
        return pl.ds(first, (c + 1) * group - first)

    def arrived(c):
        return recv_d[c * group : (c + 1) * group].reshape(rows, features + part)

    def project(c):
        wait_for(recv_d.at[span(c)], rd_sem.at[c])
        held = arrived(c)[:, :features]
        for k in range(nx):
            send_a[c, k] = dot(held, w[nx + k]).astype(BF16)
        remote(send_a.at[c], recv_a.at[c], sa_sem.at[c], ra_sem.at[c], partner)
        for k in range(nx):
            own_a[c, k] = dot(held, w[k])

    def add_partner(c):
        wait_for(recv_a.at[c], ra_sem.at[c])
        for k in range(1, nx):
            send_b[c, k - 1] = (own_a[c, k] + recv_a[c, k].astype(F32)).astype(BF16)
            remote(send_b.at[c, k - 1], recv_b.at[c, k - 1], sb_sem.at[c, k - 1], rb_sem.at[c, k - 1], along_x(k))
        own_b[c] = own_a[c, 0] + recv_a[c, 0].astype(F32)

    def activate(c):
        for k in range(1, nx):
            wait_for(recv_b.at[c, k - 1], rb_sem.at[c, k - 1])
        pre = own_b[c]
        for k in range(1, nx):
            pre = pre + recv_b[c, k - 1].astype(F32)
        gate_pre, up_pre = pre[:, :part], pre[:, part:]
        upstream = arrived(c)[:, features:].astype(F32)
        s = jax.nn.sigmoid(gate_pre)
        d_gate = upstream * up_pre * s * (1.0 + gate_pre * (1.0 - s))
        d_up = upstream * gate_pre * s
        d_pair[c, 0] = jnp.concatenate([d_gate, d_up], axis=1).astype(BF16)
        for k in range(1, nx):
            remote(d_pair.at[c, 0], d_pair.at[c, nx - k], sg_sem.at[c, k - 1], rg_sem.at[c, nx - k], along_x(k))
        remote(d_pair.at[c, 0], d_pair.at[c, nx], sh_sem.at[c, 0], rh_sem.at[c, 0], partner)
        hid[c] = (gate_pre * s * up_pre).astype(BF16)

    def forward(c):
        for k in (*range(1, nx, 2), *range(2, nx, 2)):
            wait_for(d_pair.at[c, k], rg_sem.at[c, k])
            remote(d_pair.at[c, k], d_pair.at[c, nx + k], sh_sem.at[c, k], rh_sem.at[c, k], partner)

    def give_back(c):
        for k in range(nx):
            wait_for(d_pair.at[c, nx + k], rh_sem.at[c, k])
        total = dot(d_pair[c, 0], w[0], (((1,), (1,)), ((), ())))
        for k in range(1, 2 * nx):
            total = total + dot(d_pair[c, k], w[k], (((1,), (1,)), ((), ())))
        back = jnp.concatenate([total.astype(BF16), hid[c]], axis=1).reshape(group, CAP, features + part)
        send_r[c * group : (c + 1) * group] = back
        if c == 0:
            recv_r[0:1] = back[0:1]

        @pl.loop(max(1, c * group), (c + 1) * group)
        def _(o):
            pltpu.make_async_remote_copy(
                src_ref=send_r.at[o],
                dst_ref=recv_r.at[o],
                send_sem=sr_sem.at[c],
                recv_sem=rr_sem.at[c],
                device_id=(to_source(o), mine),
                device_id_type=MESH,
            ).start()

    stages = (project, add_partner, activate, forward, give_back)
    for step in range(CHUNKS + len(stages) - 1):
        for late, stage in enumerate(stages):
            if 0 <= step - late < CHUNKS:
                stage(step - late)

    held = jnp.concatenate([arrived(c)[:, :features] for c in range(CHUNKS)], axis=0)
    out_copies = []
    for k in range(2 * nx):
        both = d_pair[:, k].reshape(CHUNKS * rows, 2 * part)
        grad[k] = dot(held, both, (((0,), (0,)), ((), ()))).astype(BF16)
        at = pl.ds(pl.multiple_of(block_of(k) * part, part), part)
        for n, target in enumerate((gg_out, gu_out)):
            copy = pltpu.make_async_copy(grad.at[k, :, pl.ds(n * part, part)], target.at[0, :, at], w_sem.at[k, n])
            copy.start()
            out_copies.append(copy)

    total = jnp.zeros((tokens, features), F32)
    hidden = jnp.zeros((pairs, part), F32)
    for c in range(CHUNKS):
        wait_for(recv_r.at[span(c)], rr_sem.at[c])
        back = recv_r[c * group : (c + 1) * group].reshape(rows, features + part)
        total = total + dot(sel_t[c], back[:, :features])
        hidden = hidden + dot(sel_pt[c], back[:, features:])
    dx_v[...] = total.astype(BF16)
    copy = pltpu.make_async_copy(dx_v, dx_out, out_sem.at[0])
    copy.start()
    out_copies.append(copy)
    hid_v[...] = hidden.astype(BF16)
    copy = pltpu.make_async_copy(hid_v, hid_out, out_sem.at[1])
    copy.start()
    out_copies.append(copy)

    for c in range(CHUNKS):
        wait_for(send_d.at[span(c)], sd_sem.at[c])
        wait_for(send_a.at[c], sa_sem.at[c])
        for k in range(1, nx):
            wait_for(send_b.at[c, k - 1], sb_sem.at[c, k - 1])
            wait_for(d_pair.at[c, 0], sg_sem.at[c, k - 1])
        for k in range(nx):
            wait_for(d_pair.at[c, k], sh_sem.at[c, k])
        wait_for(send_r.at[span(c)], sr_sem.at[c])
    for copy in out_copies:
        copy.wait()


def local(ny, nz, nx, tokens, routing, w_gate, w_up, cotangent):
    tok_rows, top = routing.shape
    features = tokens.shape[1]
    part = cotangent.shape[2]
    hidden_width = w_gate.shape[2]
    experts = ny * nz
    pairs = tok_rows * top
    rows = experts // CHUNKS * CAP
    flat = cotangent.reshape(pairs, part)
    any_ref = pl.BlockSpec(memory_space=pl.ANY)
    wide = features + part
    dma = pltpu.SemaphoreType.DMA
    hidden, dx, gg, gu = pl.pallas_call(
        functools.partial(kernel, ny, nz, nx),
        out_shape=(
            jax.ShapeDtypeStruct((pairs, part), BF16),
            jax.ShapeDtypeStruct((tok_rows, features), BF16),
            jax.ShapeDtypeStruct((1, features, hidden_width), BF16),
            jax.ShapeDtypeStruct((1, features, hidden_width), BF16),
        ),
        in_specs=[any_ref] * 5,
        out_specs=(any_ref,) * 4,
        scratch_shapes=[
            pltpu.VMEM((tok_rows, features), BF16),
            pltpu.VMEM((top, tok_rows), jnp.int32),
            pltpu.VMEM((pairs, part), BF16),
            pltpu.VMEM((2 * nx, features, 2 * part), BF16),
            pltpu.VMEM((experts, CAP, wide), BF16),
            pltpu.VMEM((experts, CAP, wide), BF16),
            pltpu.VMEM((CHUNKS, tok_rows, rows), BF16),
            pltpu.VMEM((CHUNKS, rows, pairs), BF16),
            pltpu.VMEM((CHUNKS, pairs, rows), BF16),
            pltpu.VMEM((CHUNKS, nx, rows, 2 * part), F32),
            pltpu.VMEM((CHUNKS, nx, rows, 2 * part), BF16),
            pltpu.VMEM((CHUNKS, nx, rows, 2 * part), BF16),
            pltpu.VMEM((CHUNKS, rows, 2 * part), F32),
            pltpu.VMEM((CHUNKS, nx - 1, rows, 2 * part), BF16),
            pltpu.VMEM((CHUNKS, nx - 1, rows, 2 * part), BF16),
            pltpu.VMEM((CHUNKS, 2 * nx, rows, 2 * part), BF16),
            pltpu.VMEM((experts, CAP, wide), BF16),
            pltpu.VMEM((experts, CAP, wide), BF16),
            pltpu.VMEM((CHUNKS, rows, part), BF16),
            pltpu.VMEM((2 * nx, features, 2 * part), BF16),
            pltpu.VMEM((pairs, part), BF16),
            pltpu.VMEM((tok_rows, features), BF16),
            dma((3,)),
            dma((2 * nx, 2)),
            dma((CHUNKS,)),
            dma((CHUNKS,)),
            dma((CHUNKS,)),
            dma((CHUNKS,)),
            dma((CHUNKS, nx - 1)),
            dma((CHUNKS, nx - 1)),
            dma((CHUNKS, nx - 1)),
            dma((CHUNKS, nx)),
            dma((CHUNKS, nx)),
            dma((CHUNKS, nx)),
            dma((CHUNKS,)),
            dma((CHUNKS,)),
            dma((2,)),
        ],
        compiler_params=pltpu.CompilerParams(
            collective_id=0, has_side_effects=True, vmem_limit_bytes=48 * 1024 * 1024
        ),
        name="experts",
    )(tokens, routing.T, w_gate, w_up, flat)
    return hidden.reshape(tok_rows, top, part), dx, gg, gu


def solution(mesh):
    experts, groups = mesh.shape["ep"], mesh.shape["dp"]
    ny = math.isqrt(experts)
    nz = experts // ny
    in_specs = (
        P("ep", "dp"),
        P("ep", None),
        P("ep", "dp", None),
        P("ep", "dp", None),
        P("ep", None, "dp"),
    )
    out_specs = (P("ep", None, "dp"), P("ep", "dp"), P("ep", "dp", None), P("ep", "dp", None))
    return jax.shard_map(
        functools.partial(local, ny, nz, groups // 2), mesh=mesh, in_specs=in_specs, out_specs=out_specs, check_vma=False
    )
```

```python
import functools
import math

import jax
import jax.numpy as jnp
from jax import lax
from jax.experimental import pallas as pl
from jax.experimental.pallas import tpu as pltpu
from jax.sharding import PartitionSpec as P

MESH = pl.DeviceIdType.MESH
BF16 = jnp.bfloat16
F32 = jnp.float32
CAP = 8
CHUNKS = 4
LIMIT = 60 * 1024 * 1024


def dot(a, b, dims=(((1,), (0,)), ((), ()))):
    return lax.dot_general(a, b, dims, preferred_element_type=F32)


def fold(i, n):
    c = i // 2
    return c if i % 2 == 0 else n - c if c else n // 2


def fold_vector(i, n):
    c, p = i >> 1, i & 1
    return jnp.where(p == 0, c, jnp.where(c == 0, n // 2, n - c))


def kernel(
    ny, nz, nx,
    tok_hbm, rout_hbm, wg_hbm, wu_hbm, cot_hbm,
    hid_out, dx_out, gg_out, gu_out,
    tok, rout, cot, w, send_d, recv_d, send_c, recv_c, send_h, recv_h, send_r, recv_r, sel_t, sel_pt,
    own_a, send_a, recv_a, send_f, recv_f, send_b, recv_b, d_pair,
    in_sem, w_sem, sd_sem, rd_sem, sc_sem, rc_sem, sh_sem, rh_sem, sr_sem, rr_sem,
    sa_sem, ra_sem, sf_sem, rf_sem, sb_sem, rb_sem, sg_sem, rg_sem, st_sem, rt_sem, sp_sem, rp_sem,
):
    experts = ny * nz
    tokens, features = tok.shape
    top = rout.shape[0]
    pairs, part = cot.shape
    group = experts // CHUNKS
    rows = group * CAP
    half = rows // 2
    me, mine = lax.axis_index("ep"), lax.axis_index("dp")
    y, z = me // nz, me % nz
    x, core = mine // 2, mine % 2
    partner = x * 2 + 1 - core

    def along_x(step):
        return lax.rem(x + step, nx) * 2 + core

    ahead, behind = along_x(1), along_x(nx - 1)

    def block_of(k):
        return along_x(k) if k < nx else lax.rem(x + k - nx, nx) * 2 + 1 - core

    def to_expert(o):
        dy, dz = fold(o // nz, ny), fold(o % nz, nz)
        return lax.rem(y + dy, ny) * nz + lax.rem(z + dz, nz)

    def to_source(o):
        dy, dz = fold(o // nz, ny), fold(o % nz, nz)
        return lax.rem(y + ny - dy, ny) * nz + lax.rem(z + nz - dz, nz)

    def wait_for(ref, sem):
        pltpu.make_async_copy(ref, ref, sem).wait()

    def remote(source, target, send_sem, recv_sem, device):
        pltpu.make_async_remote_copy(
            src_ref=source,
            dst_ref=target,
            send_sem=send_sem,
            recv_sem=recv_sem,
            device_id=device,
            device_id_type=MESH,
        ).start()

    def on_x(source, target, send_sem, recv_sem, device):
        remote(source, target, send_sem, recv_sem, (me, device))

    def span(c):
        first = max(1, c * group)
        return pl.ds(first, (c + 1) * group - first)

    def exchange(c, source, target, send_sem, recv_sem, where):
        for o in range(max(1, c * group), (c + 1) * group):
            remote(source.at[o], target.at[o], send_sem.at[c], recv_sem.at[c], (where(o), mine))

    def rows_of(ref, c):
        return ref[c * group : (c + 1) * group].reshape(rows, ref.shape[2])

    def put(source, target, c, value):
        value = value.astype(BF16).reshape(group, CAP, source.shape[2])
        source[c * group : (c + 1) * group] = value
        if c == 0:
            target[0:1] = value[0:1]

    small = [
        pltpu.make_async_copy(rout_hbm, rout, in_sem.at[0]),
        pltpu.make_async_copy(tok_hbm, tok, in_sem.at[1]),
        pltpu.make_async_copy(cot_hbm, cot, in_sem.at[2]),
    ]
    for copy in small:
        copy.start()
    barrier = pltpu.get_barrier_semaphore()
    for o in range(experts - 1, 0, -1):
        pl.semaphore_signal(barrier, inc=1, device_id=(to_expert(o), mine), device_id_type=MESH)
    for there in (ahead, behind, partner):
        pl.semaphore_signal(barrier, inc=1, device_id=(me, there), device_id_type=MESH)
    w_copies = []
    for k in range(2 * nx):
        at = pl.ds(pl.multiple_of(block_of(k) * part, part), part)
        for n, source in enumerate((wg_hbm, wu_hbm)):
            copy = pltpu.make_async_copy(source.at[0, :, at], w.at[k, :, pl.ds(n * part, part)], w_sem.at[k, n])
            copy.start()
            w_copies.append(copy)

    before = (
        lax.broadcasted_iota(jnp.int32, (tokens, tokens), 0) < lax.broadcasted_iota(jnp.int32, (tokens, tokens), 1)
    ).astype(F32).astype(BF16)
    small[0].wait()
    routes = rout[...]

    def experts_of(c):
        row = lax.broadcasted_iota(jnp.int32, (rows, tokens), 0)
        o = row // CAP + c * group
        dy, dz = fold_vector(o // nz, ny), fold_vector(o % nz, nz)
        return ((y + dy) & (ny - 1)) * nz + ((z + dz) & (nz - 1)), row % CAP

    sels = []
    for c in range(CHUNKS):
        expert, slot = experts_of(c)
        hit = routes[0:1, :] == expert
        for k in range(1, top):
            hit = hit | (routes[k : k + 1, :] == expert)
        hit = hit.astype(F32)
        earlier = dot(hit.astype(BF16), before)
        sels.append(jnp.where(earlier == slot.astype(F32), hit, 0.0))
        if c == 0:
            small[1].wait()
        put(send_d, recv_d, c, dot(sels[c].astype(BF16), tok[...]))
    pl.semaphore_wait(barrier, experts + 2)
    for c in range(CHUNKS):
        exchange(c, send_d, recv_d, sd_sem, rd_sem, to_expert)

    spread = (
        lax.broadcasted_iota(jnp.int32, (tokens, pairs), 1) // top == lax.broadcasted_iota(jnp.int32, (tokens, pairs), 0)
    ).astype(F32).astype(BF16)
    named = dot(routes.astype(F32).astype(BF16), spread)
    place = lax.broadcasted_iota(jnp.int32, (top, pairs), 1) % top == lax.broadcasted_iota(jnp.int32, (top, pairs), 0)
    chosen = jnp.sum(jnp.where(place, named, 0.0), axis=0, keepdims=True)
    small[2].wait()
    for c in range(CHUNKS):
        expert, _ = experts_of(c)
        expanded = dot(sels[c].astype(BF16), spread)
        sel_pair = jnp.where(chosen == expert.astype(F32)[:, 0:1], expanded, 0.0)
        put(send_c, recv_c, c, dot(sel_pair.astype(BF16), cot[...]))
        sel_t[c] = sels[c].T.astype(BF16)
        sel_pt[c] = sel_pair.T.astype(BF16)
    for copy in w_copies:
        copy.wait()

    def project(c):
        wait_for(recv_d.at[span(c)], rd_sem.at[c])
        held = rows_of(recv_d, c)
        for k in (2, 1, 3, 0):
            send_a[c, k] = dot(held, w[nx + k]).astype(BF16)
        on_x(send_a.at[c], recv_a.at[c], sa_sem.at[c], ra_sem.at[c], partner)
        for k in (2, 1, 3, 0):
            own_a[c, k] = dot(held, w[k])
        exchange(c, send_c, recv_c, sc_sem, rc_sem, to_expert)

    low, high = pl.ds(0, half), pl.ds(half, half)

    def add_partner(c):
        wait_for(recv_a.at[c], ra_sem.at[c])
        send_f[c] = (own_a[c, 2] + recv_a[c, 2].astype(F32)).astype(BF16)
        on_x(send_f.at[c, low], recv_f.at[c, low], sf_sem.at[c, 0], rf_sem.at[c, 0], ahead)
        on_x(send_f.at[c, high], recv_f.at[c, high], sf_sem.at[c, 1], rf_sem.at[c, 1], behind)
        send_b[c, 0, half:] = (own_a[c, 1, half:] + recv_a[c, 1, half:].astype(F32)).astype(BF16)
        on_x(send_b.at[c, 0, high], recv_b.at[c, 0, high], sb_sem.at[c, 0], rb_sem.at[c, 0], ahead)
        send_b[c, 1, :half] = (own_a[c, 3, :half] + recv_a[c, 3, :half].astype(F32)).astype(BF16)
        on_x(send_b.at[c, 1, low], recv_b.at[c, 1, low], sb_sem.at[c, 1], rb_sem.at[c, 1], behind)

    def relay(c):
        wait_for(recv_f.at[c, low], rf_sem.at[c, 0])
        first = own_a[c, 1, :half] + recv_a[c, 1, :half].astype(F32) + recv_f[c, :half].astype(F32)
        send_b[c, 0, :half] = first.astype(BF16)
        on_x(send_b.at[c, 0, low], recv_b.at[c, 0, low], sb_sem.at[c, 2], rb_sem.at[c, 2], ahead)
        wait_for(recv_f.at[c, high], rf_sem.at[c, 1])
        second = own_a[c, 3, half:] + recv_a[c, 3, half:].astype(F32) + recv_f[c, half:].astype(F32)
        send_b[c, 1, half:] = second.astype(BF16)
        on_x(send_b.at[c, 1, high], recv_b.at[c, 1, high], sb_sem.at[c, 3], rb_sem.at[c, 3], behind)

    def activate(c):
        wait_for(recv_b.at[c, 0, high], rb_sem.at[c, 0])
        wait_for(recv_b.at[c, 1, low], rb_sem.at[c, 1])
        wait_for(recv_b.at[c, 0, low], rb_sem.at[c, 2])
        wait_for(recv_b.at[c, 1, high], rb_sem.at[c, 3])
        pre = own_a[c, 0] + recv_a[c, 0].astype(F32) + recv_b[c, 0].astype(F32) + recv_b[c, 1].astype(F32)
        gate_pre, up_pre = pre[:, :part], pre[:, part:]
        wait_for(recv_c.at[span(c)], rc_sem.at[c])
        upstream = rows_of(recv_c, c).astype(F32)
        s = jax.nn.sigmoid(gate_pre)
        d_gate = upstream * up_pre * s * (1.0 + gate_pre * (1.0 - s))
        d_up = upstream * gate_pre * s
        d_pair[c, 0] = jnp.concatenate([d_gate, d_up], axis=1).astype(BF16)
        on_x(d_pair.at[c, 0], d_pair.at[c, nx - 1], sg_sem.at[c, 0], rg_sem.at[c, 0], ahead)
        on_x(d_pair.at[c, 0], d_pair.at[c, 1], sg_sem.at[c, 1], rg_sem.at[c, 1], behind)
        on_x(d_pair.at[c, 0], d_pair.at[c, nx], sp_sem.at[c, 0], rp_sem.at[c, 0], partner)
        put(send_h, recv_h, c, gate_pre * s * up_pre)
        exchange(c, send_h, recv_h, sh_sem, rh_sem, to_source)

    def forward(c):
        wait_for(d_pair.at[c, 3], rg_sem.at[c, 0])
        on_x(d_pair.at[c, 3, low], d_pair.at[c, 2, low], st_sem.at[c, 0], rt_sem.at[c, 0], ahead)
        on_x(d_pair.at[c, 3], d_pair.at[c, nx + 3], sp_sem.at[c, 3], rp_sem.at[c, 3], partner)
        wait_for(d_pair.at[c, 1], rg_sem.at[c, 1])
        on_x(d_pair.at[c, 1, high], d_pair.at[c, 2, high], st_sem.at[c, 1], rt_sem.at[c, 1], behind)
        on_x(d_pair.at[c, 1], d_pair.at[c, nx + 1], sp_sem.at[c, 1], rp_sem.at[c, 1], partner)

    def forward_far(c):
        wait_for(d_pair.at[c, 2, low], rt_sem.at[c, 0])
        wait_for(d_pair.at[c, 2, high], rt_sem.at[c, 1])
        on_x(d_pair.at[c, 2], d_pair.at[c, nx + 2], sp_sem.at[c, 2], rp_sem.at[c, 2], partner)

    def give_back(c):
        total = jnp.zeros((rows, features), F32)
        for k in (0, 1, 3, nx, nx + 1, nx + 3, 2, nx + 2):
            if k >= nx:
                wait_for(d_pair.at[c, k], rp_sem.at[c, k - nx])
            total = total + dot(d_pair[c, k], w[k], (((1,), (1,)), ((), ())))
        put(send_r, recv_r, c, total)
        exchange(c, send_r, recv_r, sr_sem, rr_sem, to_source)

    stages = (project, add_partner, relay, activate, forward, forward_far, give_back)
    for step in range(CHUNKS + len(stages) - 1):
        for late, stage in enumerate(stages):
            if 0 <= step - late < CHUNKS:
                stage(step - late)

    held = jnp.concatenate([rows_of(recv_d, c) for c in range(CHUNKS)], axis=0)
    for k in range(2 * nx):
        both = d_pair[:, k].reshape(CHUNKS * rows, 2 * part)
        grad = dot(held, both, (((0,), (0,)), ((), ()))).astype(BF16)
        at = pl.ds(pl.multiple_of(block_of(k) * part, part), part)
        gg_out[0, :, at] = grad[:, :part]
        gu_out[0, :, at] = grad[:, part:]

    hidden = jnp.zeros((pairs, part), F32)
    for c in range(CHUNKS):
        wait_for(recv_h.at[span(c)], rh_sem.at[c])
        hidden = hidden + dot(sel_pt[c], rows_of(recv_h, c))
    hid_out[...] = hidden.astype(BF16)
    total = jnp.zeros((tokens, features), F32)
    for c in range(CHUNKS):
        wait_for(recv_r.at[span(c)], rr_sem.at[c])
        total = total + dot(sel_t[c], rows_of(recv_r, c))
    dx_out[...] = total.astype(BF16)

    for c in range(CHUNKS):
        wait_for(send_d.at[span(c)], sd_sem.at[c])
        wait_for(send_c.at[span(c)], sc_sem.at[c])
        wait_for(send_h.at[span(c)], sh_sem.at[c])
        wait_for(send_r.at[span(c)], sr_sem.at[c])
        wait_for(send_a.at[c], sa_sem.at[c])
        for n in range(2):
            wait_for(send_f.at[c, low], sf_sem.at[c, n])
            wait_for(d_pair.at[c, 0], sg_sem.at[c, n])
            wait_for(d_pair.at[c, 0, low], st_sem.at[c, n])
        for n in range(4):
            wait_for(send_b.at[c, 0, low], sb_sem.at[c, n])
            wait_for(d_pair.at[c, n], sp_sem.at[c, n])


def finish(*refs):
    count = (len(refs) - 1) // 2
    copies = [pltpu.make_async_copy(refs[n], refs[count + n], refs[-1].at[n]) for n in range(count)]
    for copy in copies:
        copy.start()
    for copy in copies:
        copy.wait()


def local(ny, nz, nx, tokens, routing, w_gate, w_up, cotangent):
    tok_rows, top = routing.shape
    features = tokens.shape[1]
    part = cotangent.shape[2]
    hidden_width = w_gate.shape[2]
    experts = ny * nz
    pairs = tok_rows * top
    rows = experts // CHUNKS * CAP
    flat = cotangent.reshape(pairs, part)
    hbm = pl.BlockSpec(memory_space=pltpu.HBM)
    vmem = pl.BlockSpec(memory_space=pltpu.VMEM)
    dma = pltpu.SemaphoreType.DMA
    by_slot = [pltpu.VMEM((experts, CAP, width), BF16) for width in (features, part, part, features) for _ in range(2)]
    shapes = ((pairs, part), (tok_rows, features), (1, features, hidden_width), (1, features, hidden_width))
    results = pl.pallas_call(
        functools.partial(kernel, ny, nz, nx),
        out_shape=tuple(pltpu.VMEM(shape, BF16) for shape in shapes),
        in_specs=[hbm] * 5,
        out_specs=(vmem,) * 4,
        scratch_shapes=[
            pltpu.VMEM((tok_rows, features), BF16),
            pltpu.VMEM((top, tok_rows), jnp.int32),
            pltpu.VMEM((pairs, part), BF16),
            pltpu.VMEM((2 * nx, features, 2 * part), BF16),
            *by_slot,
            pltpu.VMEM((CHUNKS, tok_rows, rows), BF16),
            pltpu.VMEM((CHUNKS, pairs, rows), BF16),
            pltpu.VMEM((CHUNKS, nx, rows, 2 * part), F32),
            pltpu.VMEM((CHUNKS, nx, rows, 2 * part), BF16),
            pltpu.VMEM((CHUNKS, nx, rows, 2 * part), BF16),
            pltpu.VMEM((CHUNKS, rows, 2 * part), BF16),
            pltpu.VMEM((CHUNKS, rows, 2 * part), BF16),
            pltpu.VMEM((CHUNKS, 2, rows, 2 * part), BF16),
            pltpu.VMEM((CHUNKS, 2, rows, 2 * part), BF16),
            pltpu.VMEM((CHUNKS, 2 * nx, rows, 2 * part), BF16),
            dma((3,)),
            dma((2 * nx, 2)),
            *[dma((CHUNKS,))] * 10,
            *[dma((CHUNKS, 2))] * 2,
            *[dma((CHUNKS, 4))] * 2,
            *[dma((CHUNKS, 2))] * 4,
            *[dma((CHUNKS, 4))] * 2,
        ],
        compiler_params=pltpu.CompilerParams(
            collective_id=0, has_side_effects=True, vmem_limit_bytes=LIMIT
        ),
        name="experts",
    )(tokens, routing.T, w_gate, w_up, flat)
    hidden, dx, gg, gu = pl.pallas_call(
        finish,
        out_shape=tuple(jax.ShapeDtypeStruct(shape, BF16) for shape in shapes),
        in_specs=[pl.BlockSpec(memory_space=pl.ANY)] * 4,
        out_specs=(hbm,) * 4,
        scratch_shapes=[dma((4,))],
        compiler_params=pltpu.CompilerParams(vmem_limit_bytes=1024 * 1024),
        name="finish",
    )(*results)
    return hidden.reshape(tok_rows, top, part), dx, gg, gu


def solution(mesh):
    experts, groups = mesh.shape["ep"], mesh.shape["dp"]
    ny = math.isqrt(experts)
    nz = experts // ny
    in_specs = (
        P("ep", "dp"),
        P("ep", None),
        P("ep", "dp", None),
        P("ep", "dp", None),
        P("ep", None, "dp"),
    )
    out_specs = (P("ep", None, "dp"), P("ep", "dp"), P("ep", "dp", None), P("ep", "dp", None))
    return jax.shard_map(
        functools.partial(local, ny, nz, groups // 2), mesh=mesh, in_specs=in_specs, out_specs=out_specs, check_vma=False
    )
```

```python
import functools
import math

import jax
import jax.numpy as jnp
from jax import lax
from jax.experimental import pallas as pl
from jax.experimental.pallas import tpu as pltpu
from jax.sharding import PartitionSpec as P

MESH = pl.DeviceIdType.MESH
BF16 = jnp.bfloat16
F32 = jnp.float32
CAP = 8
CHUNKS = 4
LIMIT = 60 * 1024 * 1024


def dot(a, b, dims=(((1,), (0,)), ((), ()))):
    return lax.dot_general(a, b, dims, preferred_element_type=F32)


def offsets_of(ny, nz):
    def hops(n, size):
        return min(n, size - n)

    found = [(dy, dz) for dy in range(ny) for dz in range(nz)]
    found.sort(key=lambda d: (hops(d[0], ny) + hops(d[1], nz), abs(hops(d[0], ny) - hops(d[1], nz)), d))
    group = len(found) // CHUNKS
    return [d for c in reversed(range(CHUNKS)) for d in found[c * group : (c + 1) * group]]


def kernel(
    ny, nz, nx,
    tok_hbm, rout_hbm, wg_hbm, wu_hbm, cot_hbm,
    hid_out, dx_out, gg_out, gu_out,
    tok, rout, cot, w, send_d, recv_d, send_c, recv_c, send_h, recv_h, send_r, recv_r, sel_t, sel_pt,
    own_a, send_a, recv_a, send_f, recv_f, send_b, recv_b, d_pair,
    in_sem, w_sem, sd_sem, rd_sem, sc_sem, rc_sem, sh_sem, rh_sem, sr_sem, rr_sem,
    sa_sem, ra_sem, sf_sem, rf_sem, sb_sem, rb_sem, sg_sem, rg_sem, st_sem, rt_sem, sp_sem, rp_sem,
):
    experts = ny * nz
    tokens, features = tok.shape
    top = rout.shape[0]
    pairs, part = cot.shape
    group = experts // CHUNKS
    rows = group * CAP
    half = rows // 2
    me, mine = lax.axis_index("ep"), lax.axis_index("dp")
    y, z = me // nz, me % nz
    x, core = mine // 2, mine % 2
    partner = x * 2 + 1 - core

    def along_x(step):
        return lax.rem(x + step, nx) * 2 + core

    ahead, behind = along_x(1), along_x(nx - 1)

    def block_of(k):
        return along_x(k) if k < nx else lax.rem(x + k - nx, nx) * 2 + 1 - core

    offsets = offsets_of(ny, nz)
    own = offsets.index((0, 0))

    def to_expert(o):
        dy, dz = offsets[o]
        return lax.rem(y + dy, ny) * nz + lax.rem(z + dz, nz)

    def to_source(o):
        dy, dz = offsets[o]
        return lax.rem(y + ny - dy, ny) * nz + lax.rem(z + nz - dz, nz)

    def wait_for(ref, sem):
        pltpu.make_async_copy(ref, ref, sem).wait()

    def remote(source, target, send_sem, recv_sem, device):
        pltpu.make_async_remote_copy(
            src_ref=source,
            dst_ref=target,
            send_sem=send_sem,
            recv_sem=recv_sem,
            device_id=device,
            device_id_type=MESH,
        ).start()

    def on_x(source, target, send_sem, recv_sem, device):
        remote(source, target, send_sem, recv_sem, (me, device))

    def span(c):
        first = c * group + (c * group == own)
        return pl.ds(first, (c + 1) * group - first)

    def exchange(c, source, target, send_sem, recv_sem, where):
        for o in range(c * group + (c * group == own), (c + 1) * group):
            remote(source.at[o], target.at[o], send_sem.at[c], recv_sem.at[c], (where(o), mine))

    def rows_of(ref, c):
        return ref[c * group : (c + 1) * group].reshape(rows, ref.shape[2])

    def put(source, target, c, value):
        value = value.astype(BF16).reshape(group, CAP, source.shape[2])
        source[c * group : (c + 1) * group] = value
        if c * group == own:
            target[own : own + 1] = value[0:1]

    small = [
        pltpu.make_async_copy(rout_hbm, rout, in_sem.at[0]),
        pltpu.make_async_copy(tok_hbm, tok, in_sem.at[1]),
        pltpu.make_async_copy(cot_hbm, cot, in_sem.at[2]),
    ]
    for copy in small:
        copy.start()
    barrier = pltpu.get_barrier_semaphore()
    for o in range(experts):
        if o == own:
            continue
        pl.semaphore_signal(barrier, inc=1, device_id=(to_expert(o), mine), device_id_type=MESH)
    for there in (ahead, behind, partner):
        pl.semaphore_signal(barrier, inc=1, device_id=(me, there), device_id_type=MESH)
    w_copies = []
    for k in range(2 * nx):
        at = pl.ds(pl.multiple_of(block_of(k) * part, part), part)
        for n, source in enumerate((wg_hbm, wu_hbm)):
            copy = pltpu.make_async_copy(source.at[0, :, at], w.at[k, :, pl.ds(n * part, part)], w_sem.at[k, n])
            copy.start()
            w_copies.append(copy)

    before = (
        lax.broadcasted_iota(jnp.int32, (tokens, tokens), 0) < lax.broadcasted_iota(jnp.int32, (tokens, tokens), 1)
    ).astype(F32).astype(BF16)
    small[0].wait()
    routes = rout[...]

    def experts_of(c):
        row = lax.broadcasted_iota(jnp.int32, (rows, tokens), 0)
        dy, dz = jnp.zeros_like(row), jnp.zeros_like(row)
        for n, (ahead_y, ahead_z) in enumerate(offsets[c * group : (c + 1) * group]):
            here = row // CAP == n
            dy, dz = jnp.where(here, ahead_y, dy), jnp.where(here, ahead_z, dz)
        return ((y + dy) & (ny - 1)) * nz + ((z + dz) & (nz - 1)), row % CAP

    sels = []
    for c in range(CHUNKS):
        expert, slot = experts_of(c)
        hit = routes[0:1, :] == expert
        for k in range(1, top):
            hit = hit | (routes[k : k + 1, :] == expert)
        hit = hit.astype(F32)
        earlier = dot(hit.astype(BF16), before)
        sels.append(jnp.where(earlier == slot.astype(F32), hit, 0.0))
        if c == 0:
            small[1].wait()
        put(send_d, recv_d, c, dot(sels[c].astype(BF16), tok[...]))
    pl.semaphore_wait(barrier, experts + 2)
    for c in range(CHUNKS):
        exchange(c, send_d, recv_d, sd_sem, rd_sem, to_expert)

    spread = (
        lax.broadcasted_iota(jnp.int32, (tokens, pairs), 1) // top == lax.broadcasted_iota(jnp.int32, (tokens, pairs), 0)
    ).astype(F32).astype(BF16)
    named = dot(routes.astype(F32).astype(BF16), spread)
    place = lax.broadcasted_iota(jnp.int32, (top, pairs), 1) % top == lax.broadcasted_iota(jnp.int32, (top, pairs), 0)
    chosen = jnp.sum(jnp.where(place, named, 0.0), axis=0, keepdims=True)
    small[2].wait()
    for c in range(CHUNKS):
        expert, _ = experts_of(c)
        expanded = dot(sels[c].astype(BF16), spread)
        sel_pair = jnp.where(chosen == expert.astype(F32)[:, 0:1], expanded, 0.0)
        put(send_c, recv_c, c, dot(sel_pair.astype(BF16), cot[...]))
        sel_t[c] = sels[c].T.astype(BF16)
        sel_pt[c] = sel_pair.T.astype(BF16)
    for copy in w_copies:
        copy.wait()

    def project(c):
        wait_for(recv_d.at[span(c)], rd_sem.at[c])
        held = rows_of(recv_d, c)
        for k in (2, 1, 3, 0):
            send_a[c, k] = dot(held, w[nx + k]).astype(BF16)
        on_x(send_a.at[c], recv_a.at[c], sa_sem.at[c], ra_sem.at[c], partner)
        for k in (2, 1, 3, 0):
            own_a[c, k] = dot(held, w[k])
        exchange(c, send_c, recv_c, sc_sem, rc_sem, to_expert)

    low, high = pl.ds(0, half), pl.ds(half, half)

    def add_partner(c):
        wait_for(recv_a.at[c], ra_sem.at[c])
        send_f[c] = (own_a[c, 2] + recv_a[c, 2].astype(F32)).astype(BF16)
        on_x(send_f.at[c, low], recv_f.at[c, low], sf_sem.at[c, 0], rf_sem.at[c, 0], ahead)
        on_x(send_f.at[c, high], recv_f.at[c, high], sf_sem.at[c, 1], rf_sem.at[c, 1], behind)
        send_b[c, 0, half:] = (own_a[c, 1, half:] + recv_a[c, 1, half:].astype(F32)).astype(BF16)
        on_x(send_b.at[c, 0, high], recv_b.at[c, 0, high], sb_sem.at[c, 0], rb_sem.at[c, 0], ahead)
        send_b[c, 1, :half] = (own_a[c, 3, :half] + recv_a[c, 3, :half].astype(F32)).astype(BF16)
        on_x(send_b.at[c, 1, low], recv_b.at[c, 1, low], sb_sem.at[c, 1], rb_sem.at[c, 1], behind)

    def relay(c):
        wait_for(recv_f.at[c, low], rf_sem.at[c, 0])
        first = own_a[c, 1, :half] + recv_a[c, 1, :half].astype(F32) + recv_f[c, :half].astype(F32)
        send_b[c, 0, :half] = first.astype(BF16)
        on_x(send_b.at[c, 0, low], recv_b.at[c, 0, low], sb_sem.at[c, 2], rb_sem.at[c, 2], ahead)
        wait_for(recv_f.at[c, high], rf_sem.at[c, 1])
        second = own_a[c, 3, half:] + recv_a[c, 3, half:].astype(F32) + recv_f[c, half:].astype(F32)
        send_b[c, 1, half:] = second.astype(BF16)
        on_x(send_b.at[c, 1, high], recv_b.at[c, 1, high], sb_sem.at[c, 3], rb_sem.at[c, 3], behind)

    def activate(c):
        wait_for(recv_b.at[c, 0, high], rb_sem.at[c, 0])
        wait_for(recv_b.at[c, 1, low], rb_sem.at[c, 1])
        wait_for(recv_b.at[c, 0, low], rb_sem.at[c, 2])
        wait_for(recv_b.at[c, 1, high], rb_sem.at[c, 3])
        pre = own_a[c, 0] + recv_a[c, 0].astype(F32) + recv_b[c, 0].astype(F32) + recv_b[c, 1].astype(F32)
        gate_pre, up_pre = pre[:, :part], pre[:, part:]
        wait_for(recv_c.at[span(c)], rc_sem.at[c])
        upstream = rows_of(recv_c, c).astype(F32)
        s = jax.nn.sigmoid(gate_pre)
        d_gate = upstream * up_pre * s * (1.0 + gate_pre * (1.0 - s))
        d_up = upstream * gate_pre * s
        d_pair[c, 0] = jnp.concatenate([d_gate, d_up], axis=1).astype(BF16)
        on_x(d_pair.at[c, 0], d_pair.at[c, nx - 1], sg_sem.at[c, 0], rg_sem.at[c, 0], ahead)
        on_x(d_pair.at[c, 0], d_pair.at[c, 1], sg_sem.at[c, 1], rg_sem.at[c, 1], behind)
        on_x(d_pair.at[c, 0], d_pair.at[c, nx], sp_sem.at[c, 0], rp_sem.at[c, 0], partner)
        put(send_h, recv_h, c, gate_pre * s * up_pre)
        exchange(c, send_h, recv_h, sh_sem, rh_sem, to_source)

    def forward(c):
        wait_for(d_pair.at[c, 3], rg_sem.at[c, 0])
        on_x(d_pair.at[c, 3, low], d_pair.at[c, 2, low], st_sem.at[c, 0], rt_sem.at[c, 0], ahead)
        on_x(d_pair.at[c, 3], d_pair.at[c, nx + 3], sp_sem.at[c, 3], rp_sem.at[c, 3], partner)
        wait_for(d_pair.at[c, 1], rg_sem.at[c, 1])
        on_x(d_pair.at[c, 1, high], d_pair.at[c, 2, high], st_sem.at[c, 1], rt_sem.at[c, 1], behind)
        on_x(d_pair.at[c, 1], d_pair.at[c, nx + 1], sp_sem.at[c, 1], rp_sem.at[c, 1], partner)

    def forward_far(c):
        wait_for(d_pair.at[c, 2, low], rt_sem.at[c, 0])
        wait_for(d_pair.at[c, 2, high], rt_sem.at[c, 1])
        on_x(d_pair.at[c, 2], d_pair.at[c, nx + 2], sp_sem.at[c, 2], rp_sem.at[c, 2], partner)

    def give_back(c):
        total = jnp.zeros((rows, features), F32)
        for k in (0, 1, 3, nx, nx + 1, nx + 3, 2, nx + 2):
            if k >= nx:
                wait_for(d_pair.at[c, k], rp_sem.at[c, k - nx])
            total = total + dot(d_pair[c, k], w[k], (((1,), (1,)), ((), ())))
        put(send_r, recv_r, c, total)
        exchange(c, send_r, recv_r, sr_sem, rr_sem, to_source)

    stages = (project, add_partner, relay, activate, forward, forward_far, give_back)
    for step in range(CHUNKS + len(stages) - 1):
        for late, stage in enumerate(stages):
            if 0 <= step - late < CHUNKS:
                stage(step - late)

    held = jnp.concatenate([rows_of(recv_d, c) for c in range(CHUNKS)], axis=0)
    for k in range(2 * nx):
        both = d_pair[:, k].reshape(CHUNKS * rows, 2 * part)
        grad = dot(held, both, (((0,), (0,)), ((), ()))).astype(BF16)
        at = pl.ds(pl.multiple_of(block_of(k) * part, part), part)
        gg_out[0, :, at] = grad[:, :part]
        gu_out[0, :, at] = grad[:, part:]

    hidden = jnp.zeros((pairs, part), F32)
    for c in range(CHUNKS):
        wait_for(recv_h.at[span(c)], rh_sem.at[c])
        hidden = hidden + dot(sel_pt[c], rows_of(recv_h, c))
    hid_out[...] = hidden.astype(BF16)
    for c in range(CHUNKS):
        wait_for(send_d.at[span(c)], sd_sem.at[c])
        wait_for(send_c.at[span(c)], sc_sem.at[c])
        wait_for(send_h.at[span(c)], sh_sem.at[c])
        wait_for(send_a.at[c], sa_sem.at[c])
        for n in range(2):
            wait_for(send_f.at[c, low], sf_sem.at[c, n])
            wait_for(d_pair.at[c, 0], sg_sem.at[c, n])
            wait_for(d_pair.at[c, 0, low], st_sem.at[c, n])
        for n in range(4):
            wait_for(send_b.at[c, 0, low], sb_sem.at[c, n])
            wait_for(d_pair.at[c, n], sp_sem.at[c, n])

    total = jnp.zeros((tokens, features), F32)
    for c in range(CHUNKS):
        wait_for(recv_r.at[span(c)], rr_sem.at[c])
        total = total + dot(sel_t[c], rows_of(recv_r, c))
    dx_out[...] = total.astype(BF16)
    for c in range(CHUNKS):
        wait_for(send_r.at[span(c)], sr_sem.at[c])


def finish(*refs):
    count = (len(refs) - 1) // 2
    copies = [pltpu.make_async_copy(refs[n], refs[count + n], refs[-1].at[n]) for n in range(count)]
    for copy in copies:
        copy.start()
    for copy in copies:
        copy.wait()


def local(ny, nz, nx, tokens, routing, w_gate, w_up, cotangent):
    tok_rows, top = routing.shape
    features = tokens.shape[1]
    part = cotangent.shape[2]
    hidden_width = w_gate.shape[2]
    experts = ny * nz
    pairs = tok_rows * top
    rows = experts // CHUNKS * CAP
    flat = cotangent.reshape(pairs, part)
    hbm = pl.BlockSpec(memory_space=pltpu.HBM)
    vmem = pl.BlockSpec(memory_space=pltpu.VMEM)
    dma = pltpu.SemaphoreType.DMA
    by_slot = [pltpu.VMEM((experts, CAP, width), BF16) for width in (features, part, part, features) for _ in range(2)]
    shapes = ((pairs, part), (tok_rows, features), (1, features, hidden_width), (1, features, hidden_width))
    results = pl.pallas_call(
        functools.partial(kernel, ny, nz, nx),
        out_shape=tuple(pltpu.VMEM(shape, BF16) for shape in shapes),
        in_specs=[hbm] * 5,
        out_specs=(vmem,) * 4,
        scratch_shapes=[
            pltpu.VMEM((tok_rows, features), BF16),
            pltpu.VMEM((top, tok_rows), jnp.int32),
            pltpu.VMEM((pairs, part), BF16),
            pltpu.VMEM((2 * nx, features, 2 * part), BF16),
            *by_slot,
            pltpu.VMEM((CHUNKS, tok_rows, rows), BF16),
            pltpu.VMEM((CHUNKS, pairs, rows), BF16),
            pltpu.VMEM((CHUNKS, nx, rows, 2 * part), F32),
            pltpu.VMEM((CHUNKS, nx, rows, 2 * part), BF16),
            pltpu.VMEM((CHUNKS, nx, rows, 2 * part), BF16),
            pltpu.VMEM((CHUNKS, rows, 2 * part), BF16),
            pltpu.VMEM((CHUNKS, rows, 2 * part), BF16),
            pltpu.VMEM((CHUNKS, 2, rows, 2 * part), BF16),
            pltpu.VMEM((CHUNKS, 2, rows, 2 * part), BF16),
            pltpu.VMEM((CHUNKS, 2 * nx, rows, 2 * part), BF16),
            dma((3,)),
            dma((2 * nx, 2)),
            *[dma((CHUNKS,))] * 10,
            *[dma((CHUNKS, 2))] * 2,
            *[dma((CHUNKS, 4))] * 2,
            *[dma((CHUNKS, 2))] * 4,
            *[dma((CHUNKS, 4))] * 2,
        ],
        compiler_params=pltpu.CompilerParams(
            collective_id=0, has_side_effects=True, vmem_limit_bytes=LIMIT
        ),
        name="experts",
    )(tokens, routing.T, w_gate, w_up, flat)
    hidden, dx, gg, gu = pl.pallas_call(
        finish,
        out_shape=tuple(jax.ShapeDtypeStruct(shape, BF16) for shape in shapes),
        in_specs=[pl.BlockSpec(memory_space=pl.ANY)] * 4,
        out_specs=(hbm,) * 4,
        scratch_shapes=[dma((4,))],
        compiler_params=pltpu.CompilerParams(vmem_limit_bytes=1024 * 1024),
        name="finish",
    )(*results)
    return hidden.reshape(tok_rows, top, part), dx, gg, gu


def solution(mesh):
    experts, groups = mesh.shape["ep"], mesh.shape["dp"]
    ny = math.isqrt(experts)
    nz = experts // ny
    in_specs = (
        P("ep", "dp"),
        P("ep", None),
        P("ep", "dp", None),
        P("ep", "dp", None),
        P("ep", None, "dp"),
    )
    out_specs = (P("ep", None, "dp"), P("ep", "dp"), P("ep", "dp", None), P("ep", "dp", None))
    return jax.shard_map(
        functools.partial(local, ny, nz, groups // 2), mesh=mesh, in_specs=in_specs, out_specs=out_specs, check_vma=False
    )
```
